512 devices in a mesh: dp: 64 (over y_hi, z, core), tensor: 8 (over x, y_lo).
Axes of the slice: x: 4, y: 4 (y_hi: 2, y_lo: 2; y = y_hi * 2 + y_lo), z: 16, core: 2. Of those that a mesh axis runs over, the one named last changes fastest.
Arguments:
- hidden: bfloat16 [8192, 5120], P('dp'), may hold values from -6 to 6
- qkv_weight: bfloat16 [5120, 6144], P(('dp', 'tensor')), may hold values from -0.078125 to 0.078125
- query_gain: float32 [128], replicated, may hold values from 0.1 to 1.9
- key_gain: float32 [128], replicated, may hold values from 0.1 to 1.9
- positions: int32 [8192], replicated, may hold values from 0 to 32767, as said below
- block_mask: int32 [64, 64], replicated, may hold values from 0 to 1, as said below
Outputs:
- keys: bfloat16 [8192, 1024], P('dp', 'tensor')
- values: bfloat16 [8192, 1024], P('dp', 'tensor')
- context: bfloat16 [8192, 4096], P('dp', 'tensor')
The draws below stay inside these ranges and needn't reach their ends.
Inputs may be any that keep to these rules, and one draw needn't show every extreme that they name: `positions`: strictly increasing; position 4 i + r with 0 <= r < 4 for the i-th surviving token; the first is 0 and the last 32767. `block_mask`: 1 on the diagonal, 0 above it.
All inputs are finite; a program needn't handle non-finite values.
Results may differ from the reference program's by a relative error of at most 0.0069.
Values may be sent and summed in bfloat16 or wider, within the bound.
No kernel may reach another device: no remote copies, remote signals or barrier semaphores. Data moves between devices by JAX's collectives and lax.ppermute only.
A program may use at most 64 MiB of HBM per device.

```python
import math
import jax
import jax.numpy as jnp
from jax import lax

D = 5120
KV = 8
HD = 128
QH = 32
BLOCK = 128
GQ = 4
COLS = 6144
TOKENS = 8192
NBLK = 64


def draw_positions(key, part):
    key = jax.random.fold_in(key, 11)
    offsets = jax.random.randint(key, (TOKENS,), 0, 4)
    offsets = offsets.at[0].set(0).at[TOKENS - 1].set(3)
    return (jnp.arange(TOKENS, dtype=jnp.int32) * 4 + offsets).astype(jnp.int32)


def draw_block_mask(key, part):
    key = jax.random.fold_in(key, 23)
    random_bits = jax.random.randint(key, (NBLK, NBLK), 0, 2)
    row_index = jnp.arange(NBLK, dtype=jnp.int32)[:, None]
    col_index = jnp.arange(NBLK, dtype=jnp.int32)[None, :]
    return jnp.where(col_index < row_index, random_bits, jnp.where(col_index == row_index, 1, 0)).astype(jnp.int32)


def block_scale(stream_key, extent, cuts, least, high):
    loudness, own = 1.0, jax.random.fold_in(stream_key, 6)
    for axis_at, blocks in cuts:
        steps = jnp.exp(jax.random.uniform(jax.random.fold_in(own, axis_at), (blocks,), jnp.float32, least / len(cuts), high / len(cuts)))
        loudness = loudness * jnp.repeat(steps, extent[axis_at] // blocks).reshape([-1 if axis == axis_at else 1 for axis in range(len(extent))])
    return loudness


def bell_draw(rng, shape, deviation, bound, split=(), kind=jnp.bfloat16):
    loudness = block_scale(rng, shape, split, -0.22, 0.18) if split else 1.0
    entries = jax.random.normal(rng, shape, jnp.float32) * deviation * loudness
    return jnp.minimum(jnp.maximum(entries, -bound), bound).astype(kind)


def setup_inputs(seed: int = 0) -> dict:
    arg_keys = jax.random.split(jax.random.key(seed), 7)
    return {
        "hidden": bell_draw(arg_keys[0], (TOKENS, D), 1.0, 6.0, ((0, 64),)),
        "qkv_weight": bell_draw(arg_keys[1], (D, COLS), D ** -0.5, 0.078125, ((0, 512),)),
        "query_gain": jnp.clip(1.0 + 0.18 * jax.random.normal(arg_keys[2], (HD,), jnp.float32), 0.1, 1.9),
        "key_gain": jnp.clip(1.0 + 0.18 * jax.random.normal(arg_keys[3], (HD,), jnp.float32), 0.1, 1.9),
        "positions": draw_positions(jax.random.fold_in(arg_keys[6], 71), 0),
        "block_mask": draw_block_mask(jax.random.fold_in(arg_keys[6], 71), 0),
    }


def head_norm(inputs, gain):
    meansq = lax.optimization_barrier(jnp.mean(inputs * inputs, axis=-1, keepdims=True))
    return inputs * lax.rsqrt(meansq + 1e-06) * gain

def rotate(inputs, token_pos):
    halfway = inputs.shape[-1] // 2
    inverse = 1000000.0 ** (-(jnp.arange(halfway, dtype=jnp.float32) * 2.0) / inputs.shape[-1])
    angles = token_pos.astype(jnp.float32)[:, None] * inverse[None, :]
    angles = angles.reshape((angles.shape[0],) + (1,) * (inputs.ndim - 2) + (halfway,))
    cosine = jnp.cos(angles)
    sine = jnp.sin(angles)
    first = inputs[..., :halfway]
    second = inputs[..., halfway:]
    return jnp.concatenate([first * cosine - second * sine, second * cosine + first * sine], axis=-1)

def reference(hidden, qkv_weight, query_gain, key_gain, positions, block_mask):
    project = jnp.dot(hidden, qkv_weight, preferred_element_type=jnp.float32).reshape(TOKENS, KV, GQ + 2, HD)
    queries = lax.optimization_barrier(rotate(head_norm(project[:, :, :GQ], query_gain), positions).astype(jnp.bfloat16))
    keys = lax.optimization_barrier(rotate(head_norm(project[:, :, GQ], key_gain), positions).astype(jnp.bfloat16))
    values = lax.optimization_barrier(project[:, :, GQ + 1].astype(jnp.bfloat16))
    key_float = keys.astype(jnp.float32)
    value_float = values.astype(jnp.float32)
    scaling = 1.0 / math.sqrt(HD)

    def one_block(index):
        query_blk = lax.dynamic_slice_in_dim(queries, index * BLOCK, BLOCK, 0).astype(jnp.float32)
        query_pos = lax.dynamic_slice_in_dim(positions, index * BLOCK, BLOCK, 0)
        mask_row = lax.dynamic_index_in_dim(block_mask, index, 0, keepdims=False)
        key_live = jnp.repeat(mask_row, BLOCK) == 1
        live = key_live[None, :] & (positions[None, :] <= query_pos[:, None])
        scores = jnp.einsum('qgjd,kgd->qgjk', query_blk, key_float) * scaling
        weights = jnp.where(live[:, None, None, :], jnp.exp(scores), 0.0)
        denom = lax.optimization_barrier(jnp.sum(weights, axis=-1))
        rounded = lax.optimization_barrier(weights.astype(jnp.bfloat16)).astype(jnp.float32)
        numer = jnp.einsum('qgjk,kgd->qgjd', rounded, value_float)
        return (numer / denom[..., None]).astype(jnp.bfloat16)
    context = lax.map(one_block, jnp.arange(NBLK, dtype=jnp.int32))
    return (keys.reshape(TOKENS, KV * HD), values.reshape(TOKENS, KV * HD), context.reshape(TOKENS, QH * HD))
```

```python
import functools
import math

import jax
import jax.numpy as jnp
from jax import lax
from jax.experimental import pallas as pl
from jax.experimental.pallas import tpu as pltpu
from jax.sharding import Mesh, PartitionSpec as P

HD = 128
BLOCK = 128
GQ = 4
KV = 8
YH, ZH, ZL, CORE, X, YL = 2, 4, 4, 2, 4, 2
NZ = ZH * ZL
GROUP = YH * CORE
DP = ("yh", "zh", "zl", "c")
TENSOR = ("x", "yl")
Z = ("zh", "zl")
bf16 = jnp.bfloat16
f32 = jnp.float32


def params():
    return pltpu.CompilerParams(vmem_limit_bytes=40 * 1024 * 1024)


def swap(inputs, axis):
    return lax.ppermute(inputs, axis, [(0, 1), (1, 0)])


def from_z(inputs, offset):
    return lax.ppermute(inputs, Z, [(i, (i - offset) % NZ) for i in range(NZ)])


def norm_rope(inputs, gain, cosine, sine):
    meansq = jnp.mean(inputs * inputs, axis=-1, keepdims=True)
    normed = inputs * lax.rsqrt(meansq + 1e-06) * gain
    return normed * cosine + pltpu.roll(normed, HD // 2, 1) * sine


def kv_partial_kernel(place, h0, h1, h2, h3, weight, out):
    member = place[1]
    for rel, rows in enumerate((h0, h1, h2, h3)):
        out[member ^ rel] = jnp.dot(rows[...], weight[...], preferred_element_type=f32)


def kv_partial(place, hiddens, weight):
    tok, depth = hiddens[0].shape
    half = depth // YH
    rows = pl.BlockSpec((tok, half), lambda i, place: (0, place[0]))
    return pl.pallas_call(
        kv_partial_kernel,
        grid_spec=pltpu.PrefetchScalarGridSpec(
            num_scalar_prefetch=1,
            grid=(1,),
            in_specs=[rows] * GROUP + [pl.BlockSpec((half, HD), lambda i, place: (0, 0))],
            out_specs=pl.BlockSpec((GROUP, tok, HD), lambda i, place: (0, 0, 0)),
        ),
        out_shape=jax.ShapeDtypeStruct((GROUP, tok, HD), f32),
        compiler_params=params(),
        name="kv_partial",
    )(place, *hiddens, weight)


def kv_finish_kernel(parts, gain, cosine, sine, keys, values, both):
    key = norm_rope(parts[0] + parts[2], gain[...], cosine[0], sine[0]).astype(bf16)
    value = (parts[1] + parts[3]).astype(bf16)
    keys[...] = key
    values[...] = value
    both[:, :HD] = key
    both[:, HD:] = value


def kv_finish(parts, gain, cosine, sine):
    tok = parts.shape[1]
    return pl.pallas_call(
        kv_finish_kernel,
        out_shape=(
            jax.ShapeDtypeStruct((tok, HD), bf16),
            jax.ShapeDtypeStruct((tok, HD), bf16),
            jax.ShapeDtypeStruct((tok, 2 * HD), bf16),
        ),
        compiler_params=params(),
        name="kv_finish",
    )(parts, gain, cosine, sine)


def q_project_kernel(place, h0, h1, h2, h3, weight, gain, cosine, sine, out):
    member = place[1]
    half = h0.shape[1] // YH
    for rel, rows in enumerate((h0, h1, h2, h3)):
        total = None
        for yh in range(YH):
            part = jnp.dot(
                rows[:, yh * half : (yh + 1) * half],
                weight[:, yh].reshape(half, HD),
                preferred_element_type=f32,
            )
            total = part if total is None else total + part
        out[member ^ rel] = norm_rope(total, gain[...], cosine[rel], sine[rel]).astype(bf16)


def q_project(place, hiddens, weight, gain, cosine, sine):
    tok, depth = hiddens[0].shape

    def whole(shape):
        return pl.BlockSpec(shape, lambda i, place: (0,) * len(shape))

    return pl.pallas_call(
        q_project_kernel,
        grid_spec=pltpu.PrefetchScalarGridSpec(
            num_scalar_prefetch=1,
            grid=(1,),
            in_specs=[whole((tok, depth))] * GROUP
            + [whole(weight.shape), whole(gain.shape), whole(cosine.shape), whole(sine.shape)],
            out_specs=whole((GROUP, tok, HD)),
        ),
        out_shape=jax.ShapeDtypeStruct((GROUP, tok, HD), bf16),
        compiler_params=params(),
        name="q_project",
    )(place, *hiddens, weight, gain, cosine, sine)


CHUNK = 2 * BLOCK
CHUNKS = [
    (0, 0, 0, 0),
    (0, CHUNK, 0, 2),
    (1, 0, 1, 0),
    (1, CHUNK, 1, 2),
    (2, 0, -1, 0),
    (2, CHUNK, -1, 2),
    (3, 0, 2, 0),
    (4, 0, 2, 2),
]


def attend_kernel(place, block_mask, query, kv0, kv1, kv2, kv3, kv4, out, numer, total):
    group = pl.program_id(0)
    yh, zh, zl, core = place[0], place[2], place[3], place[4]
    query_block = (group // CORE) * (NZ * CORE) + (zh * ZL + zl) * CORE + lax.rem(group, CORE)
    rows = query[...].reshape(GQ * BLOCK, HD)
    ahead = lax.broadcasted_iota(jnp.int32, (GQ * BLOCK, BLOCK), 1) - lax.rem(
        lax.broadcasted_iota(jnp.int32, (GQ * BLOCK, BLOCK), 0), BLOCK
    )
    numer[...] = jnp.zeros_like(numer)
    total[...] = jnp.zeros_like(total)
    refs = (kv0, kv1, kv2, kv3, kv4)
    for which, start, offset, zh0 in CHUNKS:
        limits = []
        for i in range(CHUNK // BLOCK):
            z_at = (zh0 + i) * ZL + lax.rem(zl + offset + ZL, ZL)
            key_block = yh * (NZ * CORE) + z_at * CORE + core
            live = (block_mask[query_block, key_block] == 1) & (key_block <= query_block)
            limits.append(
                jnp.where(live, jnp.where(key_block == query_block, 0, 2 * BLOCK), -2 * BLOCK)
            )

        @pl.when(jnp.maximum(limits[0], limits[1]) >= 0)
        def _(which=which, start=start, limits=limits):
            keys = refs[which][start : start + CHUNK, :HD]
            values = refs[which][start : start + CHUNK, HD:]
            scores = lax.dot_general(
                rows, keys, (((1,), (1,)), ((), ())), preferred_element_type=f32
            )
            raised = jnp.exp(scores * (1.0 / math.sqrt(HD)))
            parts = [
                jnp.where(ahead <= limits[i], raised[:, i * BLOCK : (i + 1) * BLOCK], 0.0)
                for i in range(CHUNK // BLOCK)
            ]
            total[...] += parts[0] + parts[1]
            weights = jnp.concatenate([p.astype(bf16) for p in parts], axis=1)
            numer[...] += jnp.dot(weights, values, preferred_element_type=f32)

    denom = jnp.sum(total[...], axis=1, keepdims=True)
    lane = lax.broadcasted_iota(jnp.int32, (BLOCK, HD), 1)
    tail = jnp.zeros((BLOCK, HD), f32)
    for head in range(GQ):
        mine = denom[head * BLOCK : (head + 1) * BLOCK]
        high = mine.astype(bf16).astype(f32)
        tail = jnp.where(lane == 2 * head, high, tail)
        tail = jnp.where(lane == 2 * head + 1, mine - high, tail)
        out[0, :, head * HD : (head + 1) * HD] = numer[
            head * BLOCK : (head + 1) * BLOCK
        ].astype(bf16)
    out[0, :, GQ * HD :] = tail.astype(bf16)


def attend(place, block_mask, query, gathered):
    tok = query.shape[2]
    rows = GQ * tok
    width = (GQ + 1) * HD

    def whole(array):
        return pl.BlockSpec(array.shape, lambda i, *_: (0,) * array.ndim)

    return pl.pallas_call(
        attend_kernel,
        grid_spec=pltpu.PrefetchScalarGridSpec(
            num_scalar_prefetch=2,
            grid=(GROUP,),
            in_specs=[pl.BlockSpec((GQ, 1, tok, HD), lambda i, *_: (0, i, 0, 0))]
            + [whole(a) for a in gathered],
            out_specs=pl.BlockSpec((1, tok, width), lambda i, *_: (i, 0, 0)),
            scratch_shapes=[pltpu.VMEM((rows, HD), f32), pltpu.VMEM((rows, BLOCK), f32)],
        ),
        out_shape=jax.ShapeDtypeStruct((GROUP, tok, width), bf16),
        compiler_params=params(),
        name="attend",
    )(place, block_mask, query, *gathered)


def combine_kernel(parts, out):
    tail = sum(parts[i, :, GQ * HD :].astype(f32) for i in range(GROUP))
    for head in range(GQ):
        at = slice(head * HD, (head + 1) * HD)
        numer = sum(parts[i, :, at].astype(f32) for i in range(GROUP))
        denom = tail[:, 2 * head : 2 * head + 1] + tail[:, 2 * head + 1 : 2 * head + 2]
        out[:, at] = (numer / denom).astype(bf16)


def combine(parts):
    return pl.pallas_call(
        combine_kernel,
        out_shape=jax.ShapeDtypeStruct((parts.shape[1], GQ * HD), bf16),
        compiler_params=params(),
        name="combine",
    )(parts)


def local(hidden, qkv_weight, query_gain, key_gain, positions, block_mask):
    tok, depth = hidden.shape
    share = qkv_weight.shape[0]
    yh, zh, zl, core = (lax.axis_index(a) for a in DP)
    member = yh * CORE + core
    place = jnp.stack([yh, member, zh, zl, core]).astype(jnp.int32)

    near = swap(hidden, "c")

    with jax.named_scope("weights"):
        split = qkv_weight.reshape(share, KV, GQ + 2, HD).transpose(2, 1, 0, 3)
        send = jnp.concatenate(
            [split[:GQ], jnp.concatenate([split[GQ:]] * YH, axis=0)], axis=-1
        ).reshape(GROUP * KV, share, 2 * HD)
        got = lax.all_to_all(send, ("yh", "c", "x", "yl"), 0, 0)
        rows = CORE * KV * share
        got, sent = lax.optimization_barrier((got, hidden))
        far = swap(sent, "yh")
        q_rows = got[:, :, :HD].reshape(YH * rows, HD)
        kv_rows = lax.dynamic_index_in_dim(
            got.reshape(YH, CORE * KV, share, 2 * HD), yh, 0, keepdims=False
        )[:, :, HD:].reshape(rows, HD)
        q_weight = lax.all_gather(q_rows, Z, axis=0, tiled=False)
        q_weight = q_weight.reshape(NZ, YH, rows, HD)
        kv_weight = lax.all_gather(kv_rows, Z, axis=0, tiled=True)

    far, _ = lax.optimization_barrier((far, kv_weight))
    hiddens = (hidden, near, far, swap(far, "c"))

    inverse = 1000000.0 ** (-(jnp.arange(HD // 2, dtype=f32) * 2.0) / HD)
    own = []
    for rel in range(GROUP):
        first = ((yh ^ (rel // CORE)) * NZ + zh * ZL + zl) * CORE + (core ^ (rel % CORE))
        own.append(lax.dynamic_slice_in_dim(positions, first * tok, tok, 0))
    angles = jnp.stack(own).astype(f32)[:, :, None] * inverse
    cosine, sine = jnp.cos(angles), jnp.sin(angles)
    cosine = jnp.concatenate([cosine, cosine], axis=-1)
    sine = jnp.concatenate([-sine, sine], axis=-1)

    with jax.named_scope("keys_values"):
        parts = kv_partial(place, hiddens, kv_weight)
        parts = lax.all_to_all(parts, ("yh", "c"), 0, 0)
        keys, values, both = kv_finish(parts, key_gain.reshape(1, HD), cosine, sine)
        line = lax.all_gather(both, "zh", axis=0, tiled=True)
        half = line.shape[0] // 2
        gathered = (
            line,
            from_z(line, 1),
            from_z(line, -1),
            from_z(line[:half], 2),
            from_z(line[half:], -2),
        )

    with jax.named_scope("queries"):
        q_weight, _ = lax.optimization_barrier((q_weight, line))
        query = q_project(place, hiddens, q_weight, query_gain.reshape(1, HD), cosine, sine)
        query = lax.all_gather(query, ("yh", "c"), axis=0, tiled=False)

    with jax.named_scope("context"):
        partial = attend(place, block_mask, query, gathered)
        partial = lax.all_to_all(partial, ("yh", "c"), 0, 0)
        context = combine(partial)
    return keys, values, context


def solution(mesh):
    fine = Mesh(mesh.devices.reshape(YH, ZH, ZL, CORE, X, YL), DP[:3] + ("c",) + TENSOR)
    return jax.shard_map(
        local,
        mesh=fine,
        in_specs=(P(DP, None), P(DP + TENSOR, None), P(), P(), P(), P()),
        out_specs=(P(DP, TENSOR), P(DP, TENSOR), P(DP, TENSOR)),
        check_vma=False,
    )
```

```python
import functools
import math

import jax
import jax.numpy as jnp
from jax import lax
from jax.experimental import pallas as pl
from jax.experimental.pallas import tpu as pltpu
from jax.sharding import Mesh, PartitionSpec as P

HD = 128
BLOCK = 128
GQ = 4
KV = 8
YH, ZH, ZL, CORE, X, YL = 2, 4, 4, 2, 4, 2
NZ = ZH * ZL
GROUP = YH * CORE
DP = ("yh", "zh", "zl", "c")
TENSOR = ("x", "yl")
Z = ("zh", "zl")
bf16 = jnp.bfloat16
f32 = jnp.float32


def params():
    return pltpu.CompilerParams(vmem_limit_bytes=24 * 1024 * 1024)


def swap(inputs, axis):
    return lax.ppermute(inputs, axis, [(0, 1), (1, 0)])


def from_z(inputs, offset):
    return lax.ppermute(inputs, Z, [(i, (i - offset) % NZ) for i in range(NZ)])


def from_z_both(inputs, offset):
    pairs = [
        (i * CORE + core, (i - (1 - 2 * core) * offset) % NZ * CORE + core)
        for i in range(NZ)
        for core in range(CORE)
    ]
    return lax.ppermute(inputs, Z + ("c",), pairs)


def norm_rope(inputs, gain, cosine, sine):
    meansq = jnp.mean(inputs * inputs, axis=-1, keepdims=True)
    normed = inputs * lax.rsqrt(meansq + 1e-06) * gain
    return normed * cosine + pltpu.roll(normed, HD // 2, 1) * sine


def kv_partial_kernel(place, h0, h1, h2, h3, weight, out):
    member = place[1]
    half = weight.shape[0]
    columns = pl.ds(pl.multiple_of(place[0] * half, half), half)
    for rel, rows in enumerate((h0, h1, h2, h3)):
        out[member ^ rel] = jnp.dot(rows[:, columns], weight[...], preferred_element_type=f32)


def specs(count):
    scalars = pl.BlockSpec(memory_space=pltpu.SMEM)
    return [scalars] + [pl.BlockSpec(memory_space=pltpu.VMEM)] * count


def kv_partial(place, hiddens, weight):
    tok = hiddens[0].shape[0]
    return pl.pallas_call(
        kv_partial_kernel,
        in_specs=specs(GROUP + 1),
        out_shape=jax.ShapeDtypeStruct((GROUP, tok, HD), f32),
        compiler_params=params(),
        name="kv_partial",
    )(place, *hiddens, weight)


def kv_finish_kernel(parts, gain, cosine, sine, keys, values, both):
    key = norm_rope(parts[0] + parts[2], gain[...], cosine[0], sine[0]).astype(bf16)
    value = (parts[1] + parts[3]).astype(bf16)
    keys[...] = key
    values[...] = value
    both[:, :HD] = key
    both[:, HD:] = value


def kv_finish(parts, gain, cosine, sine):
    tok = parts.shape[1]
    return pl.pallas_call(
        kv_finish_kernel,
        out_shape=(
            jax.ShapeDtypeStruct((tok, HD), bf16),
            jax.ShapeDtypeStruct((tok, HD), bf16),
            jax.ShapeDtypeStruct((tok, 2 * HD), bf16),
        ),
        compiler_params=params(),
        name="kv_finish",
    )(parts, gain, cosine, sine)


def q_project_kernel(place, h0, h1, h2, h3, weight, gain, cosine, sine, out):
    member = place[1]
    half = h0.shape[1] // YH
    for rel, rows in enumerate((h0, h1, h2, h3)):
        total = None
        for yh in range(YH):
            part = jnp.dot(
                rows[:, yh * half : (yh + 1) * half],
                weight[:, yh].reshape(half, HD),
                preferred_element_type=f32,
            )
            total = part if total is None else total + part
        out[member ^ rel] = norm_rope(total, gain[...], cosine[rel], sine[rel]).astype(bf16)


def q_project(place, hiddens, weight, gain, cosine, sine):
    tok = hiddens[0].shape[0]
    return pl.pallas_call(
        q_project_kernel,
        in_specs=specs(GROUP + 4),
        out_shape=jax.ShapeDtypeStruct((GROUP, tok, HD), bf16),
        compiler_params=params(),
        name="q_project",
    )(place, *hiddens, weight, gain, cosine, sine)


OFFSETS = (0, 1, -1, 2)
BATCH = 4
WIDTH = (GQ + 1) * HD
LOW = 64


def query_member(place, remote, i):
    yh = 1 - place[0] if remote else place[0]
    return yh, jnp.where(i == 0, 1 - place[4], place[4])


def attend_kernel(remote, place, block_mask, query, *refs):
    lines = refs[: len(OFFSETS)]
    out, key_value, numer, total, slot_at, limit_at, sems = refs[len(OFFSETS) :]
    step = pl.program_id(0)
    yh, zh, zl, core = place[0], place[2], place[3], place[4]
    line_rows = ZH * BLOCK
    copies = [
        pltpu.make_async_copy(line, key_value.at[pl.ds(i * line_rows, line_rows)], sems.at[i])
        for i, line in enumerate(lines)
    ]

    @pl.when(step == 0)
    def _():
        for copy in copies:
            copy.start()

    query_yh, query_core = query_member(place, remote, step)
    query_block = query_yh * (NZ * CORE) + (zh * ZL + zl) * CORE + query_core
    slots = len(OFFSETS) * ZH
    for i in range(slots + BATCH):
        slot_at[i] = jnp.int32(0)
        limit_at[i] = jnp.int32(-2 * BLOCK)
    count = jnp.int32(0)
    for i in range(slots):
        z_at = (i % ZH) * ZL + lax.rem(zl + (OFFSETS[i // ZH] + ZL), ZL)
        key_block = yh * (NZ * CORE) + z_at * CORE + core
        live = (block_mask[query_block, key_block] == 1) & (key_block <= query_block)
        slot_at[count] = jnp.int32(i)
        limit_at[count] = jnp.where(
            live, jnp.where(key_block == query_block, 0, 2 * BLOCK), -2 * BLOCK
        )
        count = count + live.astype(jnp.int32)

    rows = query[...].reshape(GQ * BLOCK, HD)
    ahead = lax.broadcasted_iota(jnp.int32, (GQ * BLOCK, BLOCK), 1) - lax.rem(
        lax.broadcasted_iota(jnp.int32, (GQ * BLOCK, BLOCK), 0), BLOCK
    )
    numer[...] = jnp.zeros_like(numer)
    total[...] = jnp.zeros_like(total)

    @pl.when(step == 0)
    def _():
        for copy in copies:
            copy.wait()

    def batch(at, carry):
        first = at * BATCH
        starts = [pl.multiple_of(slot_at[first + i] * BLOCK, BLOCK) for i in range(BATCH)]
        limits = [limit_at[first + i] for i in range(BATCH)]
        block = jnp.concatenate([key_value[pl.ds(x, BLOCK), :] for x in starts], axis=0)
        scores = lax.dot_general(
            rows, block[:, :HD], (((1,), (1,)), ((), ())), preferred_element_type=f32
        )
        raised = jnp.exp2(scores * (math.log2(math.e) / math.sqrt(HD)))
        parts = [
            jnp.where(ahead <= limits[i], raised[:, i * BLOCK : (i + 1) * BLOCK], 0.0)
            for i in range(BATCH)
        ]
        total[...] += (parts[0] + parts[1]) + (parts[2] + parts[3])
        weights = jnp.concatenate([p.astype(bf16) for p in parts], axis=1)
        numer[...] += jnp.dot(weights, block[:, HD:], preferred_element_type=f32)
        return carry

    lax.fori_loop(0, (count + BATCH - 1) // BATCH, batch, 0)

    denom = jnp.sum(total[...], axis=1, keepdims=True)
    lane = lax.broadcasted_iota(jnp.int32, (BLOCK, HD), 1)
    tail = jnp.zeros((BLOCK, HD), f32)
    for head in range(GQ):
        mine = denom[head * BLOCK : (head + 1) * BLOCK]
        if remote:
            high = mine.astype(bf16).astype(f32)
            tail = jnp.where(lane == head, high, tail)
            tail = jnp.where(lane == head + LOW, mine - high, tail)
        else:
            tail = jnp.where(lane == head, mine, tail)
        out[0, :, head * HD : (head + 1) * HD] = numer[
            head * BLOCK : (head + 1) * BLOCK
        ].astype(out.dtype)
    out[0, :, GQ * HD :] = tail.astype(out.dtype)


def attend(remote, place, block_mask, query, lines):
    tok = query.shape[2]
    rows = GQ * tok
    keys = sum(line.shape[0] for line in lines)

    def of_query(i, place, block_mask):
        yh, core = query_member(place, remote, i)
        return 0, yh * CORE + core, 0, 0

    slots = len(OFFSETS) * ZH + BATCH
    return pl.pallas_call(
        functools.partial(attend_kernel, remote),
        grid_spec=pltpu.PrefetchScalarGridSpec(
            num_scalar_prefetch=2,
            grid=(CORE,),
            in_specs=[pl.BlockSpec((GQ, 1, tok, HD), of_query)]
            + [pl.BlockSpec(memory_space=pl.ANY)] * len(lines),
            out_specs=pl.BlockSpec((1, tok, WIDTH), lambda i, *_: (i, 0, 0)),
            scratch_shapes=[
                pltpu.VMEM((keys, 2 * HD), bf16),
                pltpu.VMEM((rows, HD), f32),
                pltpu.VMEM((rows, BLOCK), f32),
                pltpu.SMEM((slots,), jnp.int32),
                pltpu.SMEM((slots,), jnp.int32),
                pltpu.SemaphoreType.DMA((len(lines),)),
            ],
        ),
        out_shape=jax.ShapeDtypeStruct((CORE, tok, WIDTH), bf16 if remote else f32),
        compiler_params=params(),
        cost_estimate=pl.CostEstimate(
            flops=4 * CORE * rows * keys * HD,
            bytes_accessed=4 * keys * HD,
            transcendentals=CORE * rows * keys,
        ),
        name="attend_remote" if remote else "attend_local",
    )(place, block_mask, query, *lines)


def fold_kernel(mine, far, out):
    out[...] = mine[0] + far[0].astype(f32)


def fold(mine, far):
    return pl.pallas_call(
        fold_kernel,
        out_shape=jax.ShapeDtypeStruct(mine.shape[1:], f32),
        compiler_params=params(),
        name="fold",
    )(mine, far)


def combine_kernel(mine, far, near, out):
    tail = mine[1, :, GQ * HD :] + far[1, :, GQ * HD :].astype(f32) + near[:, GQ * HD :]
    for head in range(GQ):
        at = slice(head * HD, (head + 1) * HD)
        numer = mine[1, :, at] + far[1, :, at].astype(f32) + near[:, at]
        denom = tail[:, head : head + 1] + tail[:, head + LOW : head + LOW + 1]
        out[:, at] = (numer / denom).astype(bf16)


def combine(mine, far, near):
    return pl.pallas_call(
        combine_kernel,
        out_shape=jax.ShapeDtypeStruct((mine.shape[1], GQ * HD), bf16),
        compiler_params=params(),
        name="combine",
    )(mine, far, near)


def local(hidden, qkv_weight, query_gain, key_gain, positions, block_mask):
    tok, depth = hidden.shape
    share = qkv_weight.shape[0]
    yh, zh, zl, core = (lax.axis_index(a) for a in DP)
    member = yh * CORE + core
    place = jnp.stack([yh, member, zh, zl, core]).astype(jnp.int32)

    near = swap(hidden, "c")

    with jax.named_scope("weights"):
        split = qkv_weight.reshape(share, KV, GQ + 2, HD).transpose(2, 1, 0, 3)
        send = jnp.concatenate(
            [split[:GQ], jnp.concatenate([split[GQ:]] * YH, axis=0)], axis=-1
        ).reshape(GROUP * KV, share, 2 * HD)
        got = lax.all_to_all(send, ("yh", "c", "x", "yl"), 0, 0)
        rows = CORE * KV * share
        got, sent = lax.optimization_barrier((got, hidden))
        far = swap(sent, "yh")
        q_rows = got[:, :, :HD].reshape(YH * rows, HD)
        kv_rows = lax.dynamic_index_in_dim(
            got.reshape(YH, CORE * KV, share, 2 * HD), yh, 0, keepdims=False
        )[:, :, HD:].reshape(rows, HD)
        q_weight = lax.all_gather(q_rows, Z, axis=0, tiled=False)
        q_weight = q_weight.reshape(NZ, YH, rows, HD)
        kv_weight = lax.all_gather(kv_rows, Z, axis=0, tiled=True)

    far, _ = lax.optimization_barrier((far, kv_weight))
    hiddens = (hidden, near, far, swap(far, "c"))

    inverse = 1000000.0 ** (-(jnp.arange(HD // 2, dtype=f32) * 2.0) / HD)
    own = []
    for rel in range(GROUP):
        first = ((yh ^ (rel // CORE)) * NZ + zh * ZL + zl) * CORE + (core ^ (rel % CORE))
        own.append(lax.dynamic_slice_in_dim(positions, first * tok, tok, 0))
    angles = jnp.stack(own).astype(f32)[:, :, None] * inverse
    cosine, sine = jnp.cos(angles), jnp.sin(angles)
    cosine = jnp.concatenate([cosine, cosine], axis=-1)
    sine = jnp.concatenate([-sine, sine], axis=-1)

    with jax.named_scope("keys_values"):
        parts = kv_partial(place, hiddens, kv_weight)
        parts = lax.all_to_all(parts, ("yh", "c"), 0, 0)
        keys, values, both = kv_finish(parts, key_gain.reshape(1, HD), cosine, sine)
        line = lax.all_gather(both, "zh", axis=0, tiled=True)
        across = from_z_both(line, 2)
        gathered = (line, from_z(line, 1), from_z(line, -1), across)

    with jax.named_scope("queries"):
        q_weight, _ = lax.optimization_barrier((q_weight, line))
        query = q_project(place, hiddens, q_weight, query_gain.reshape(1, HD), cosine, sine)
        query = lax.all_gather(query, ("yh", "c"), axis=0, tiled=False)

    with jax.named_scope("context"):
        remote = attend(True, place, block_mask, query, gathered)
        far_part = lax.ppermute(remote, "yh", [(0, 1)])
        mine = attend(False, place, block_mask, query, gathered)
        near_part = swap(fold(mine, far_part), "c")
        context = combine(mine, far_part, near_part)
    return keys, values, context


def solution(mesh):
    fine = Mesh(mesh.devices.reshape(YH, ZH, ZL, CORE, X, YL), DP[:3] + ("c",) + TENSOR)
    return jax.shard_map(
        local,
        mesh=fine,
        in_specs=(P(DP, None), P(DP + TENSOR, None), P(), P(), P(), P()),
        out_specs=(P(DP, TENSOR), P(DP, TENSOR), P(DP, TENSOR)),
        check_vma=False,
    )
```

```python
import functools
import math

import jax
import jax.numpy as jnp
from jax import lax
from jax.experimental import pallas as pl
from jax.experimental.pallas import tpu as pltpu
from jax.sharding import Mesh, PartitionSpec as P

HD = 128
BLOCK = 128
GQ = 4
PAIR = 2
KV = 8
YH, ZH, ZL, CORE, X, YL = 2, 4, 4, 2, 4, 2
NZ = ZH * ZL
GROUP = YH * CORE
DP = ("yh", "zh", "zl", "c")
TENSOR = ("x", "yl")
Z = ("zh", "zl")
bf16 = jnp.bfloat16
f32 = jnp.float32


def params():
    return pltpu.CompilerParams(vmem_limit_bytes=24 * 1024 * 1024)


def swap(inputs, axis):
    return lax.ppermute(inputs, axis, [(0, 1), (1, 0)])


def from_z(inputs, offset):
    return lax.ppermute(inputs, Z, [(i, (i - offset) % NZ) for i in range(NZ)])


def from_z_both(inputs, offset):
    pairs = [
        (i * CORE + core, (i - (1 - 2 * core) * offset) % NZ * CORE + core)
        for i in range(NZ)
        for core in range(CORE)
    ]
    return lax.ppermute(inputs, Z + ("c",), pairs)


def norm_rope(inputs, gain, cosine, sine):
    meansq = jnp.mean(inputs * inputs, axis=-1, keepdims=True)
    normed = inputs * lax.rsqrt(meansq + 1e-06) * gain
    return normed * cosine + pltpu.roll(normed, HD // 2, 1) * sine


def specs(count):
    scalars = pl.BlockSpec(memory_space=pltpu.SMEM)
    return [scalars] + [pl.BlockSpec(memory_space=pltpu.VMEM)] * count


def pack_kernel(weight, out):
    for yh in range(YH):
        for core in range(CORE):
            for head in range(KV):
                first = head * (GQ + 2)
                slots = [first + yh * PAIR + core, first + GQ + core]
                for i, slot in enumerate(slots):
                    out[(yh * CORE + core) * KV + head, :, i * HD : (i + 1) * HD] = weight[
                        :, slot * HD : (slot + 1) * HD
                    ]


def pack(weight):
    return pl.pallas_call(
        pack_kernel,
        out_shape=jax.ShapeDtypeStruct(
            (GROUP * KV, weight.shape[0], 2 * HD), weight.dtype
        ),
        compiler_params=params(),
        name="pack",
    )(weight)


def half_dots(place, h0, h1, weight):
    half = weight.shape[0]
    columns = pl.ds(pl.multiple_of(place[0] * half, half), half)
    return [
        jnp.dot(rows[:, columns], weight[...], preferred_element_type=f32) for rows in (h0, h1)
    ]


def kv_first_kernel(place, h0, h1, weight, out):
    out[0], out[1] = half_dots(place, h0, h1, weight)


def kv_first(place, hiddens, weight):
    tok = hiddens[0].shape[0]
    return pl.pallas_call(
        kv_first_kernel,
        in_specs=specs(YH + 1),
        out_shape=jax.ShapeDtypeStruct((YH, tok, HD), f32),
        compiler_params=params(),
        name="kv_first",
    )(place, *hiddens, weight)


def kv_second_kernel(place, h0, h1, weight, first, keep, send):
    core = place[4]
    mine = pl.ds(pl.multiple_of(core * HD, HD), HD)
    other = pl.ds(pl.multiple_of((1 - core) * HD, HD), HD)
    dots = half_dots(place, h0, h1, weight)
    for rel, out in enumerate((keep, send)):
        out[:, mine] = first[rel]
        out[:, other] = dots[rel]


def kv_second(place, hiddens, weight, first):
    tok = hiddens[0].shape[0]
    shape = jax.ShapeDtypeStruct((tok, 2 * HD), f32)
    return pl.pallas_call(
        kv_second_kernel,
        in_specs=specs(YH + 2),
        out_shape=(shape, shape),
        compiler_params=params(),
        name="kv_second",
    )(place, *hiddens, weight, first)


def kv_finish_kernel(place, keep, sent, gain, cosine, sine, keys, values, both):
    total = keep[...] + sent[1 - place[0]]
    key = norm_rope(total[:, :HD], gain[...], cosine[0], sine[0]).astype(bf16)
    value = total[:, HD:].astype(bf16)
    keys[...] = key
    values[...] = value
    both[:, :HD] = key
    both[:, HD:] = value


def kv_finish(place, keep, sent, gain, cosine, sine):
    tok = keep.shape[0]
    return pl.pallas_call(
        kv_finish_kernel,
        in_specs=specs(5),
        out_shape=(
            jax.ShapeDtypeStruct((tok, HD), bf16),
            jax.ShapeDtypeStruct((tok, HD), bf16),
            jax.ShapeDtypeStruct((tok, 2 * HD), bf16),
        ),
        compiler_params=params(),
        name="kv_finish",
    )(place, keep, sent, gain, cosine, sine)


def q_project_kernel(place, h0, h1, mine, other, gain, cosine, sine, out):
    yh, core = place[0], place[4]
    half = h0.shape[1] // YH
    for flip, weight in enumerate((mine, other)):
        for rel, rows in enumerate((h0, h1)):
            total = None
            for i in range(YH):
                part = jnp.dot(
                    rows[:, i * half : (i + 1) * half],
                    weight[:, i].reshape(half, HD),
                    preferred_element_type=f32,
                )
                total = part if total is None else total + part
            out[core ^ flip, yh ^ rel] = norm_rope(
                total, gain[...], cosine[rel], sine[rel]
            ).astype(bf16)


def q_project(place, hiddens, weights, gain, cosine, sine):
    tok = hiddens[0].shape[0]
    return pl.pallas_call(
        q_project_kernel,
        in_specs=specs(YH + CORE + 3),
        out_shape=jax.ShapeDtypeStruct((PAIR, YH, tok, HD), bf16),
        compiler_params=params(),
        name="q_project",
    )(place, *hiddens, *weights, gain, cosine, sine)


OFFSETS = (0, 1, -1, 2)
BATCH = 4
WIDTH = (GQ + 1) * HD
LOW = 64


def query_member(place, remote, i):
    yh = 1 - place[0] if remote else place[0]
    return yh, jnp.where(i == 0, 1 - place[4], place[4])


def attend_kernel(remote, place, block_mask, query, *refs):
    lines = refs[: len(OFFSETS)]
    peer, own, key_value, numer, total, slot_at, limit_at, sems = refs[-8:]
    step = pl.program_id(0)
    yh, zh, zl, core = place[0], place[2], place[3], place[4]
    line_rows = ZH * BLOCK
    copies = [
        pltpu.make_async_copy(line, key_value.at[pl.ds(i * line_rows, line_rows)], sems.at[i])
        for i, line in enumerate(lines)
    ]

    @pl.when(step == 0)
    def _():
        for copy in copies:
            copy.start()

    query_yh, query_core = query_member(place, remote, step)
    query_block = query_yh * (NZ * CORE) + (zh * ZL + zl) * CORE + query_core
    slots = len(OFFSETS) * ZH
    for i in range(slots + BATCH):
        slot_at[i] = jnp.int32(0)
        limit_at[i] = jnp.int32(-2 * BLOCK)
    count = jnp.int32(0)
    for i in range(slots):
        z_at = (i % ZH) * ZL + lax.rem(zl + (OFFSETS[i // ZH] + ZL), ZL)
        key_block = yh * (NZ * CORE) + z_at * CORE + core
        live = (block_mask[query_block, key_block] == 1) & (key_block <= query_block)
        slot_at[count] = jnp.int32(i)
        limit_at[count] = jnp.where(
            live, jnp.where(key_block == query_block, 0, 2 * BLOCK), -2 * BLOCK
        )
        count = count + live.astype(jnp.int32)

    rows = query[...].reshape(GQ * BLOCK, HD)
    ahead = lax.broadcasted_iota(jnp.int32, (GQ * BLOCK, BLOCK), 1) - lax.rem(
        lax.broadcasted_iota(jnp.int32, (GQ * BLOCK, BLOCK), 0), BLOCK
    )
    numer[...] = jnp.zeros_like(numer)
    total[...] = jnp.zeros_like(total)

    @pl.when(step == 0)
    def _():
        for copy in copies:
            copy.wait()

    def batch(at, carry):
        first = at * BATCH
        starts = [pl.multiple_of(slot_at[first + i] * BLOCK, BLOCK) for i in range(BATCH)]
        limits = [limit_at[first + i] for i in range(BATCH)]
        block = jnp.concatenate([key_value[pl.ds(x, BLOCK), :] for x in starts], axis=0)
        scores = lax.dot_general(
            rows, block[:, :HD], (((1,), (1,)), ((), ())), preferred_element_type=f32
        )
        raised = jnp.exp2(scores * (math.log2(math.e) / math.sqrt(HD)))
        parts = [
            jnp.where(ahead <= limits[i], raised[:, i * BLOCK : (i + 1) * BLOCK], 0.0)
            for i in range(BATCH)
        ]
        total[...] += (parts[0] + parts[1]) + (parts[2] + parts[3])
        weights = jnp.concatenate([p.astype(bf16) for p in parts], axis=1)
        numer[...] += jnp.dot(weights, block[:, HD:], preferred_element_type=f32)
        return carry

    lax.fori_loop(0, (count + BATCH - 1) // BATCH, batch, 0)

    denom = jnp.sum(total[...], axis=1, keepdims=True)
    lane = lax.broadcasted_iota(jnp.int32, (BLOCK, HD), 1)
    tail = jnp.zeros((BLOCK, HD), f32)
    for head in range(GQ):
        tail = jnp.where(lane == head, denom[head * BLOCK : (head + 1) * BLOCK], tail)
    for at, out in enumerate((peer, own)):

        @pl.when(step == at)
        def _(out=out):
            for head in range(GQ):
                out[:, head * HD : (head + 1) * HD] = numer[
                    head * BLOCK : (head + 1) * BLOCK
                ].astype(out.dtype)
            out[:, GQ * HD :] = tail if out.dtype == f32 else two_words(tail)


def two_words(denom):
    high = denom.astype(bf16).astype(f32)
    return (high + pltpu.roll(denom - high, LOW, 1)).astype(bf16)


def attend(remote, place, block_mask, query, lines, after=()):
    tok = query.shape[-2]
    rows = GQ * tok
    keys = sum(line.shape[0] for line in lines)

    def of_query(i, place, block_mask):
        yh, core = query_member(place, remote, i)
        return 0, core, 0, yh, 0, 0

    slots = len(OFFSETS) * ZH + BATCH
    return pl.pallas_call(
        functools.partial(attend_kernel, remote),
        grid_spec=pltpu.PrefetchScalarGridSpec(
            num_scalar_prefetch=2,
            grid=(CORE,),
            in_specs=[pl.BlockSpec((YH, 1, PAIR, 1, tok, HD), of_query)]
            + [pl.BlockSpec(memory_space=pl.ANY)] * (len(lines) + len(after)),
            out_specs=(pl.BlockSpec((tok, WIDTH), lambda i, *_: (0, 0)),) * CORE,
            scratch_shapes=[
                pltpu.VMEM((keys, 2 * HD), bf16),
                pltpu.VMEM((rows, HD), f32),
                pltpu.VMEM((rows, BLOCK), f32),
                pltpu.SMEM((slots,), jnp.int32),
                pltpu.SMEM((slots,), jnp.int32),
                pltpu.SemaphoreType.DMA((len(lines),)),
            ],
        ),
        out_shape=(
            jax.ShapeDtypeStruct((tok, WIDTH), f32 if remote else bf16),
            jax.ShapeDtypeStruct((tok, WIDTH), f32),
        ),
        compiler_params=params(),
        cost_estimate=pl.CostEstimate(
            flops=4 * CORE * rows * keys * HD,
            bytes_accessed=4 * keys * HD,
            transcendentals=CORE * rows * keys,
        ),
        name="attend_remote" if remote else "attend_local",
    )(place, block_mask, query, *lines, *after)


def fold_kernel(place, own, both, out):
    got = both.at[1 - place[4]]
    out[:, : GQ * HD] = (own[:, : GQ * HD] + got[:, : GQ * HD]).astype(bf16)
    out[:, GQ * HD :] = two_words(own[:, GQ * HD :] + got[:, GQ * HD :])


def fold(place, own, both):
    return pl.pallas_call(
        fold_kernel,
        in_specs=specs(2),
        out_shape=jax.ShapeDtypeStruct(own.shape, bf16),
        compiler_params=params(),
        name="fold",
    )(place, own, both)


def combine_kernel(place, own, both, far, out):
    got = both.at[1 - place[4]]
    tail = own[:, GQ * HD :] + got[:, GQ * HD :].astype(f32) + far[:, GQ * HD :].astype(f32)
    for head in range(GQ):
        at = slice(head * HD, (head + 1) * HD)
        numer = own[:, at] + got[:, at].astype(f32) + far[:, at].astype(f32)
        denom = tail[:, head : head + 1] + tail[:, head + LOW : head + LOW + 1]
        out[:, at] = (numer / denom).astype(bf16)


def combine(place, own, both, far):
    return pl.pallas_call(
        combine_kernel,
        in_specs=specs(3),
        out_shape=jax.ShapeDtypeStruct((own.shape[0], GQ * HD), bf16),
        compiler_params=params(),
        name="combine",
    )(place, own, both, far)


def local(hidden, qkv_weight, query_gain, key_gain, positions, block_mask):
    tok, depth = hidden.shape
    share = qkv_weight.shape[0]
    yh, zh, zl, core = (lax.axis_index(a) for a in DP)
    place = jnp.stack([yh, yh * CORE + core, zh, zl, core]).astype(jnp.int32)

    with jax.named_scope("weights"):
        got = lax.all_to_all(pack(qkv_weight), ("yh", "c", "x", "yl"), 0, 0)
        got, sent = lax.optimization_barrier((got, hidden))
        far = swap(sent, "yh")
        rows = CORE * KV * share
        q_rows = got[:, :, :HD].reshape(YH * rows, HD)
        kv_rows = lax.dynamic_index_in_dim(
            got.reshape(YH, CORE * KV, share, 2 * HD), yh, 0, keepdims=False
        )[:, :, HD:].reshape(rows, HD)
        q_weight = lax.all_gather(q_rows, Z, axis=0, tiled=False)
        q_weight = q_weight.reshape(NZ, YH, rows, HD)
        kv_weight = lax.all_gather(kv_rows, Z, axis=0, tiled=True)

    hiddens = (hidden, far)

    inverse = 1000000.0 ** (-(jnp.arange(HD // 2, dtype=f32) * 2.0) / HD)
    own = []
    for rel in range(YH):
        first = ((yh ^ rel) * NZ + zh * ZL + zl) * CORE + core
        own.append(lax.dynamic_slice_in_dim(positions, first * tok, tok, 0))
    angles = jnp.stack(own).astype(f32)[:, :, None] * inverse
    cosine, sine = jnp.cos(angles), jnp.sin(angles)
    cosine = jnp.concatenate([cosine, cosine], axis=-1)
    sine = jnp.concatenate([-sine, sine], axis=-1)

    with jax.named_scope("keys_values"):
        other = swap(kv_weight, "c")
        first = kv_first(place, hiddens, kv_weight)
        keep, send = kv_second(place, hiddens, other, first)
        sent = lax.all_gather(send, "yh", axis=0, tiled=False)
        keys, values, both = kv_finish(
            place, keep, sent, key_gain.reshape(1, HD), cosine, sine
        )
        line = lax.all_gather(both, "zh", axis=0, tiled=True)
        line, q_weight = lax.optimization_barrier((line, q_weight))
        q_other = swap(q_weight, "c")
        across = from_z_both(line, 2)
        gathered = (line, from_z(line, 1), from_z(line, -1), across)

    with jax.named_scope("queries"):
        query = q_project(place, hiddens, (q_weight, q_other), query_gain.reshape(1, HD), cosine, sine)
        query = lax.all_gather(query, ("yh", "c"), axis=0, tiled=False)
        query = query.reshape(YH, CORE, PAIR, YH, tok, HD)

    with jax.named_scope("context"):
        peer, own = attend(True, place, block_mask, query, gathered)
        both = lax.all_gather(peer, "c", axis=0, tiled=False)
        folded = fold(place, own, both)
        far_part = lax.ppermute(folded, "yh", [(0, 1)])
        peer, own = attend(False, place, block_mask, query, gathered, (folded,))
        both = lax.all_gather(peer, "c", axis=0, tiled=False)
        context = combine(place, own, both, far_part)
    return keys, values, context


def solution(mesh):
    fine = Mesh(mesh.devices.reshape(YH, ZH, ZL, CORE, X, YL), DP[:3] + ("c",) + TENSOR)
    return jax.shard_map(
        local,
        mesh=fine,
        in_specs=(P(DP, None), P(DP + TENSOR, None), P(), P(), P(), P()),
        out_specs=(P(DP, TENSOR), P(DP, TENSOR), P(DP, TENSOR)),
        check_vma=False,
    )
```

```python
import functools
import math

import jax
import jax.numpy as jnp
from jax import lax
from jax.experimental import pallas as pl
from jax.experimental.pallas import tpu as pltpu
from jax.sharding import Mesh, PartitionSpec as P

HD = 128
BLOCK = 128
GQ = 4
PAIR = 2
KV = 8
YH, ZH, ZL, CORE, X, YL = 2, 4, 4, 2, 4, 2
NZ = ZH * ZL
GROUP = YH * CORE
DP = ("yh", "zh", "zl", "c")
TENSOR = ("x", "yl")
Z = ("zh", "zl")
bf16 = jnp.bfloat16
f32 = jnp.float32


def params():
    return pltpu.CompilerParams(vmem_limit_bytes=24 * 1024 * 1024)


def swap(inputs, axis):
    return lax.ppermute(inputs, axis, [(0, 1), (1, 0)])


def from_z(inputs, offset):
    return lax.ppermute(inputs, Z, [(i, (i - offset) % NZ) for i in range(NZ)])


def from_z_both(inputs, offset):
    pairs = [
        (i * CORE + core, (i - (1 - 2 * core) * offset) % NZ * CORE + core)
        for i in range(NZ)
        for core in range(CORE)
    ]
    return lax.ppermute(inputs, Z + ("c",), pairs)


def norm_rope(inputs, gain, cosine, sine):
    meansq = jnp.mean(inputs * inputs, axis=-1, keepdims=True)
    normed = inputs * lax.rsqrt(meansq + 1e-06) * gain
    return normed * cosine + pltpu.roll(normed, HD // 2, 1) * sine


def pack_kernel(weight, out):
    for yh in range(YH):
        for head in range(KV):
            first = head * (GQ + 2)
            for i, slot in enumerate((first + yh * PAIR, first + GQ)):
                out[yh * KV + head, :, i * PAIR * HD : (i + 1) * PAIR * HD] = weight[
                    :, slot * HD : (slot + PAIR) * HD
                ]


def pack(weight):
    return pl.pallas_call(
        pack_kernel,
        out_shape=jax.ShapeDtypeStruct(
            (YH * KV, weight.shape[0], 2 * PAIR * HD), weight.dtype
        ),
        compiler_params=params(),
        name="pack",
    )(weight)


def kv_partial_kernel(h0, h1, mine, other, keep, send, weight):
    core = lax.axis_index("c")
    nz, _, share, wide = weight.shape
    half = nz * CORE * share
    weight[:, core] = mine[...].reshape(nz, share, wide)
    weight[:, 1 - core] = other[...].reshape(nz, share, wide)
    columns = pl.ds(pl.multiple_of(lax.axis_index("yh") * half, half), half)
    whole = weight[...].reshape(half, wide)
    for rows, out in ((h0, keep), (h1, send)):
        out[...] = jnp.dot(rows[:, columns], whole, preferred_element_type=f32)


def kv_partial(hiddens, mine, other):
    tok = hiddens[0].shape[0]
    shape = jax.ShapeDtypeStruct((tok, 2 * HD), f32)
    return pl.pallas_call(
        kv_partial_kernel,
        out_shape=(shape, shape),
        scratch_shapes=[pltpu.VMEM((NZ, CORE, mine.shape[0] // NZ, mine.shape[1]), bf16)],
        compiler_params=params(),
        name="kv_partial",
    )(*hiddens, mine, other)


def kv_finish_kernel(keep, sent, gain, cosine, sine, keys, values, both):
    total = keep[...] + sent[1 - lax.axis_index("yh")]
    key = norm_rope(total[:, :HD], gain[...], cosine[0], sine[0]).astype(bf16)
    value = total[:, HD:].astype(bf16)
    keys[...] = key
    values[...] = value
    both[:, :HD] = key
    both[:, HD:] = value


def kv_finish(keep, sent, gain, cosine, sine):
    tok = keep.shape[0]
    return pl.pallas_call(
        kv_finish_kernel,
        out_shape=(
            jax.ShapeDtypeStruct((tok, HD), bf16),
            jax.ShapeDtypeStruct((tok, HD), bf16),
            jax.ShapeDtypeStruct((tok, 2 * HD), bf16),
        ),
        compiler_params=params(),
        name="kv_finish",
    )(keep, sent, gain, cosine, sine)


def q_project_kernel(h0, h1, gain, cosine, sine, mine, other, out, weight, sem):
    yh, core = lax.axis_index("yh"), lax.axis_index("c")
    half = h0.shape[1] // YH
    copies = [
        pltpu.make_async_copy(source.at[:, i], weight.at[i, :, owner], sem.at[i, flip])
        for i in range(YH)
        for flip, (source, owner) in enumerate(((mine, core), (other, 1 - core)))
    ]
    for copy in copies:
        copy.start()
    totals = [None] * YH
    for i in range(YH):
        for copy in copies[i * CORE : (i + 1) * CORE]:
            copy.wait()
        columns = weight[i].reshape(half, PAIR * HD)
        for rel, rows in enumerate((h0, h1)):
            part = jnp.dot(
                rows[:, i * half : (i + 1) * half], columns, preferred_element_type=f32
            )
            totals[rel] = part if i == 0 else totals[rel] + part
    for rel, total in enumerate(totals):
        for head in range(PAIR):
            out[head, yh ^ rel] = norm_rope(
                total[:, head * HD : (head + 1) * HD], gain[...], cosine[rel], sine[rel]
            ).astype(bf16)


def q_project(hiddens, weights, gain, cosine, sine):
    tok = hiddens[0].shape[0]
    nz, halves, share, wide = weights[0].shape
    return pl.pallas_call(
        q_project_kernel,
        in_specs=[pl.BlockSpec(memory_space=pltpu.VMEM)] * (YH + 3)
        + [pl.BlockSpec(memory_space=pl.ANY)] * CORE,
        out_shape=jax.ShapeDtypeStruct((PAIR, YH, tok, HD), bf16),
        scratch_shapes=[
            pltpu.VMEM((halves, nz, CORE, share, wide), bf16),
            pltpu.SemaphoreType.DMA((halves, CORE)),
        ],
        compiler_params=params(),
        name="q_project",
    )(*hiddens, gain, cosine, sine, *weights)


OFFSETS = (0, 1, -1, 2)
BATCH = 4
WIDTH = (GQ + 1) * HD
LOW = 64


def attend_kernel(remote, masks, query, *refs):
    lines = refs[: len(OFFSETS)]
    peer, own, key_value, numer, total, limit_at = refs[-6:]
    yh, zh, zl, core = (lax.axis_index(a) for a in DP)
    query_yh = 1 - yh if remote else yh
    ahead = lax.broadcasted_iota(jnp.int32, (GQ * BLOCK, BLOCK), 1) - lax.rem(
        lax.broadcasted_iota(jnp.int32, (GQ * BLOCK, BLOCK), 0), BLOCK
    )
    lane = lax.broadcasted_iota(jnp.int32, (BLOCK, HD), 1)
    for query_core, out in ((1 - core, peer), (core, own)):
        query_block = query_yh * (NZ * CORE) + (zh * ZL + zl) * CORE + query_core
        count = jnp.int32(0)
        for i, offset in enumerate(OFFSETS):
            for j in range(ZH):
                z_at = j * ZL + lax.rem(zl + (offset + ZL), ZL)
                key_block = yh * (NZ * CORE) + z_at * CORE + core
                live = (masks[query_core, key_block] == 1) & (key_block <= query_block)

                @pl.when(live)
                def _(i=i, j=j, count=count, key_block=key_block, query_block=query_block):
                    there = pl.ds(pl.multiple_of(count * BLOCK, BLOCK), BLOCK)
                    key_value[there, :] = lines[i][j * BLOCK : (j + 1) * BLOCK, :]
                    limit_at[count] = jnp.where(key_block == query_block, 0, 2 * BLOCK)

                count = count + live.astype(jnp.int32)
        for i in range(BATCH - 1):
            there = pl.ds(pl.multiple_of((count + i) * BLOCK, BLOCK), BLOCK)
            key_value[there, :] = lines[0][:BLOCK, :]
            limit_at[count + i] = jnp.int32(-2 * BLOCK)

        rows = query[:, query_core, :, query_yh].reshape(GQ * BLOCK, HD)
        numer[...] = jnp.zeros_like(numer)
        total[...] = jnp.zeros_like(total)

        def batch(at, carry):
            first = at * BATCH
            limits = [limit_at[first + i] for i in range(BATCH)]
            there = pl.ds(pl.multiple_of(first * BLOCK, BATCH * BLOCK), BATCH * BLOCK)
            scores = lax.dot_general(
                rows,
                key_value[there, :HD],
                (((1,), (1,)), ((), ())),
                preferred_element_type=f32,
            )
            raised = jnp.exp2(scores * (math.log2(math.e) / math.sqrt(HD)))
            parts = [
                jnp.where(ahead <= limits[i], raised[:, i * BLOCK : (i + 1) * BLOCK], 0.0)
                for i in range(BATCH)
            ]
            total[...] += (parts[0] + parts[1]) + (parts[2] + parts[3])
            weights = jnp.concatenate([p.astype(bf16) for p in parts], axis=1)
            numer[...] += jnp.dot(weights, key_value[there, HD:], preferred_element_type=f32)
            return carry

        lax.fori_loop(0, (count + BATCH - 1) // BATCH, batch, 0)

        denom = jnp.sum(total[...], axis=1, keepdims=True)
        tail = jnp.zeros((BLOCK, HD), f32)
        for head in range(GQ):
            at = slice(head * BLOCK, (head + 1) * BLOCK)
            tail = jnp.where(lane == head, denom[at], tail)
            out[:, head * HD : (head + 1) * HD] = numer[at].astype(out.dtype)
        out[:, GQ * HD :] = tail if out.dtype == f32 else two_words(tail)


def two_words(denom):
    high = denom.astype(bf16).astype(f32)
    return (high + pltpu.roll(denom - high, LOW, 1)).astype(bf16)


def attend(remote, masks, query, lines, after=()):
    tok = query.shape[-2]
    rows = GQ * tok
    blocks = len(OFFSETS) * ZH + BATCH - 1
    in_vmem = pl.BlockSpec(memory_space=pltpu.VMEM)
    return pl.pallas_call(
        functools.partial(attend_kernel, remote),
        in_specs=[pl.BlockSpec(memory_space=pltpu.SMEM)]
        + [in_vmem] * (1 + len(lines))
        + [pl.BlockSpec(memory_space=pl.ANY)] * len(after),
        scratch_shapes=[
            pltpu.VMEM((blocks * BLOCK, 2 * HD), bf16),
            pltpu.VMEM((rows, HD), f32),
            pltpu.VMEM((rows, BLOCK), f32),
            pltpu.SMEM((blocks,), jnp.int32),
        ],
        out_shape=(
            jax.ShapeDtypeStruct((tok, WIDTH), f32 if remote else bf16),
            jax.ShapeDtypeStruct((tok, WIDTH), f32),
        ),
        compiler_params=params(),
        cost_estimate=pl.CostEstimate(
            flops=4 * CORE * rows * blocks * BLOCK * HD,
            bytes_accessed=4 * blocks * BLOCK * HD,
            transcendentals=CORE * rows * blocks * BLOCK,
        ),
        name="attend_remote" if remote else "attend_local",
    )(masks, query, *lines, *after)


def fold_kernel(own, both, out):
    got = both.at[1 - lax.axis_index("c")]
    out[:, : GQ * HD] = (own[:, : GQ * HD] + got[:, : GQ * HD]).astype(bf16)
    out[:, GQ * HD :] = two_words(own[:, GQ * HD :] + got[:, GQ * HD :])


def fold(own, both):
    return pl.pallas_call(
        fold_kernel,
        out_shape=jax.ShapeDtypeStruct(own.shape, bf16),
        compiler_params=params(),
        name="fold",
    )(own, both)


def combine_kernel(own, both, far, out):
    got = both.at[1 - lax.axis_index("c")]
    tail = own[:, GQ * HD :] + got[:, GQ * HD :].astype(f32) + far[:, GQ * HD :].astype(f32)
    for head in range(GQ):
        at = slice(head * HD, (head + 1) * HD)
        numer = own[:, at] + got[:, at].astype(f32) + far[:, at].astype(f32)
        denom = tail[:, head : head + 1] + tail[:, head + LOW : head + LOW + 1]
        out[:, at] = (numer / denom).astype(bf16)


def combine(own, both, far):
    return pl.pallas_call(
        combine_kernel,
        out_shape=jax.ShapeDtypeStruct((own.shape[0], GQ * HD), bf16),
        compiler_params=params(),
        name="combine",
    )(own, both, far)


def local(hidden, qkv_weight, query_gain, key_gain, positions, block_mask):
    tok, depth = hidden.shape
    share = qkv_weight.shape[0]
    yh, zh, zl, core = (lax.axis_index(a) for a in DP)
    with jax.named_scope("weights"):
        got = lax.all_to_all(pack(qkv_weight), ("yh", "x", "yl"), 0, 0)
        got, sent = lax.optimization_barrier((got, hidden))
        far = swap(sent, "yh")
        rows, wide = KV * share, PAIR * HD
        q_rows = got[:, :, :wide].reshape(YH * rows, wide)
        kv_rows = lax.dynamic_index_in_dim(
            got.reshape(YH, KV, share, 2 * wide), yh, 0, keepdims=False
        )[:, :, wide:].reshape(rows, wide)
        q_weight = lax.all_gather(q_rows, Z, axis=0, tiled=False)
        q_weight = q_weight.reshape(NZ, YH, rows, wide)
        kv_weight = lax.all_gather(kv_rows, Z, axis=0, tiled=True)

    hiddens = (hidden, far)

    inverse = 1000000.0 ** (-(jnp.arange(HD // 2, dtype=f32) * 2.0) / HD)
    own = []
    for rel in range(YH):
        first = ((yh ^ rel) * NZ + zh * ZL + zl) * CORE + core
        own.append(lax.dynamic_slice_in_dim(positions, first * tok, tok, 0))
    angles = jnp.stack(own).astype(f32)[:, :, None] * inverse
    cosine, sine = jnp.cos(angles), jnp.sin(angles)
    cosine = jnp.concatenate([cosine, cosine], axis=-1)
    sine = jnp.concatenate([-sine, sine], axis=-1)

    with jax.named_scope("keys_values"):
        keep, send = kv_partial(hiddens, kv_weight, swap(kv_weight, "c"))
        sent = lax.all_gather(send, "yh", axis=0, tiled=False)
        keys, values, both = kv_finish(
            keep, sent, key_gain.reshape(1, HD), cosine, sine
        )
        line = lax.all_gather(both, "zh", axis=0, tiled=True)
        line, q_weight = lax.optimization_barrier((line, q_weight))
        q_other = swap(q_weight, "c")
        across = from_z_both(line, 2)
        gathered = (line, from_z(line, 1), from_z(line, -1), across)

    with jax.named_scope("queries"):
        query = q_project(hiddens, (q_weight, q_other), query_gain.reshape(1, HD), cosine, sine)
        query = lax.all_gather(query, ("yh", "c"), axis=0, tiled=False)
        query = query.reshape(YH, CORE, PAIR, YH, tok, HD)

    def masks(query_yh):
        first = (query_yh * NZ + zh * ZL + zl) * CORE
        return lax.dynamic_slice_in_dim(block_mask, first, CORE, 0)

    with jax.named_scope("context"):
        peer, own = attend(True, masks(1 - yh), query, gathered)
        both = lax.all_gather(peer, "c", axis=0, tiled=False)
        folded = fold(own, both)
        far_part = lax.ppermute(folded, "yh", [(0, 1)])
        peer, own = attend(False, masks(yh), query, gathered, (folded,))
        both = lax.all_gather(peer, "c", axis=0, tiled=False)
        context = combine(own, both, far_part)
    return keys, values, context


def solution(mesh):
    fine = Mesh(mesh.devices.reshape(YH, ZH, ZL, CORE, X, YL), DP[:3] + ("c",) + TENSOR)
    return jax.shard_map(
        local,
        mesh=fine,
        in_specs=(P(DP, None), P(DP + TENSOR, None), P(), P(), P(), P()),
        out_specs=(P(DP, TENSOR), P(DP, TENSOR), P(DP, TENSOR)),
        check_vma=False,
    )
```

```python
import functools
import math

import jax
import jax.numpy as jnp
from jax import lax
from jax.experimental import pallas as pl
from jax.experimental.pallas import tpu as pltpu
from jax.sharding import Mesh, PartitionSpec as P

HD = 128
BLOCK = 128
GQ = 4
PAIR = 2
KV = 8
YH, ZH, ZL, CORE, X, YL = 2, 4, 4, 2, 4, 2
NZ = ZH * ZL
GROUP = YH * CORE
DP = ("yh", "zh", "zl", "c")
TENSOR = ("x", "yl")
Z = ("zh", "zl")
bf16 = jnp.bfloat16
f32 = jnp.float32


ALTERNATE = [[z * CORE + (z + first) % CORE for z in range(NZ)] for first in range(CORE)]


def params():
    return pltpu.CompilerParams(vmem_limit_bytes=24 * 1024 * 1024)


def swap(inputs, axis):
    return lax.ppermute(inputs, axis, [(0, 1), (1, 0)])


def from_z(inputs, offset):
    return lax.ppermute(inputs, Z, [(i, (i - offset) % NZ) for i in range(NZ)])


def from_z_both(inputs, offset):
    pairs = [
        (i * CORE + core, (i - (1 - 2 * core) * offset) % NZ * CORE + core)
        for i in range(NZ)
        for core in range(CORE)
    ]
    return lax.ppermute(inputs, Z + ("c",), pairs)


def norm_rope(inputs, gain, cosine, sine):
    meansq = jnp.mean(inputs * inputs, axis=-1, keepdims=True)
    normed = inputs * lax.rsqrt(meansq + 1e-06) * gain
    return normed * cosine + pltpu.roll(normed, HD // 2, 1) * sine


def pack_kernel(weight, out):
    for yh in range(YH):
        for head in range(KV):
            first = head * (GQ + 2)
            for i, slot in enumerate((first + yh * PAIR, first + GQ)):
                out[yh * KV + head, :, i * PAIR * HD : (i + 1) * PAIR * HD] = weight[
                    :, slot * HD : (slot + PAIR) * HD
                ]


def pack(weight):
    return pl.pallas_call(
        pack_kernel,
        out_shape=jax.ShapeDtypeStruct(
            (YH * KV, weight.shape[0], 2 * PAIR * HD), weight.dtype
        ),
        compiler_params=params(),
        name="pack",
    )(weight)


def kv_partial_kernel(h0, h1, mine, other, keep, send, weight):
    core = lax.axis_index("c")
    pairs, _, _, share, wide = weight.shape
    nz = 2 * pairs
    half = nz * CORE * share
    even = lax.rem(core + lax.axis_index("zl"), 2)
    for source, first in ((mine, even), (other, 1 - even)):
        chunks = source[...].reshape(nz // 2, 2, share, wide)
        weight[:, 0, first] = chunks[:, 0]
        weight[:, 1, 1 - first] = chunks[:, 1]
    columns = pl.ds(pl.multiple_of(lax.axis_index("yh") * half, half), half)
    whole = weight[...].reshape(half, wide)
    for rows, out in ((h0, keep), (h1, send)):
        out[...] = jnp.dot(rows[:, columns], whole, preferred_element_type=f32)


def kv_partial(hiddens, mine, other):
    tok = hiddens[0].shape[0]
    shape = jax.ShapeDtypeStruct((tok, 2 * HD), f32)
    return pl.pallas_call(
        kv_partial_kernel,
        out_shape=(shape, shape),
        scratch_shapes=[pltpu.VMEM((NZ // 2, 2, CORE, mine.shape[0] // NZ, mine.shape[1]), bf16)],
        compiler_params=params(),
        name="kv_partial",
    )(*hiddens, mine, other)


def kv_finish_kernel(keep, sent, gain, cosine, sine, keys, values, both):
    total = keep[...] + sent[1 - lax.axis_index("yh")]
    key = norm_rope(total[:, :HD], gain[...], cosine[0], sine[0]).astype(bf16)
    value = total[:, HD:].astype(bf16)
    keys[...] = key
    values[...] = value
    both[:, :HD] = key
    both[:, HD:] = value


def kv_finish(keep, sent, gain, cosine, sine):
    tok = keep.shape[0]
    return pl.pallas_call(
        kv_finish_kernel,
        out_shape=(
            jax.ShapeDtypeStruct((tok, HD), bf16),
            jax.ShapeDtypeStruct((tok, HD), bf16),
            jax.ShapeDtypeStruct((tok, 2 * HD), bf16),
        ),
        compiler_params=params(),
        name="kv_finish",
    )(keep, sent, gain, cosine, sine)


def q_project_kernel(h0, h1, gain, cosine, sine, weight, out):
    yh = lax.axis_index("yh")
    half = h0.shape[1] // YH
    totals = [None] * YH
    for i in range(YH):
        columns = weight[:, :, i].reshape(half, PAIR * HD)
        for rel, rows in enumerate((h0, h1)):
            part = jnp.dot(
                rows[:, i * half : (i + 1) * half], columns, preferred_element_type=f32
            )
            totals[rel] = part if i == 0 else totals[rel] + part
    for rel, total in enumerate(totals):
        for head in range(PAIR):
            out[head, yh ^ rel] = norm_rope(
                total[:, head * HD : (head + 1) * HD], gain[...], cosine[rel], sine[rel]
            ).astype(bf16)


def q_project(hiddens, weight, gain, cosine, sine):
    tok = hiddens[0].shape[0]
    return pl.pallas_call(
        q_project_kernel,
        out_shape=jax.ShapeDtypeStruct((PAIR, YH, tok, HD), bf16),
        compiler_params=params(),
        name="q_project",
    )(*hiddens, gain, cosine, sine, weight)


OFFSETS = (0, 1, -1, 2)
BATCH = 4
WIDTH = (GQ + 1) * HD
LOW = 64


def attend_kernel(remote, masks, query, *refs):
    lines = refs[: len(OFFSETS)]
    peer, own, key_value, numer, total, limit_at = refs[-6:]
    yh, zh, zl, core = (lax.axis_index(a) for a in DP)
    query_yh = 1 - yh if remote else yh
    ahead = lax.broadcasted_iota(jnp.int32, (GQ * BLOCK, BLOCK), 1) - lax.rem(
        lax.broadcasted_iota(jnp.int32, (GQ * BLOCK, BLOCK), 0), BLOCK
    )
    lane = lax.broadcasted_iota(jnp.int32, (BLOCK, HD), 1)
    for query_core, out in ((1 - core, peer), (core, own)):
        query_block = query_yh * (NZ * CORE) + (zh * ZL + zl) * CORE + query_core
        count = jnp.int32(0)
        for i, offset in enumerate(OFFSETS):
            for j in range(ZH):
                z_at = j * ZL + lax.rem(zl + (offset + ZL), ZL)
                key_block = yh * (NZ * CORE) + z_at * CORE + core
                live = (masks[query_yh * CORE + query_core, key_block] == 1) & (key_block <= query_block)

                @pl.when(live)
                def _(i=i, j=j, count=count, key_block=key_block, query_block=query_block):
                    there = pl.ds(pl.multiple_of(count * BLOCK, BLOCK), BLOCK)
                    key_value[there, :] = lines[i][j * BLOCK : (j + 1) * BLOCK, :]
                    limit_at[count] = jnp.where(key_block == query_block, 0, 2 * BLOCK)

                count = count + live.astype(jnp.int32)
        for i in range(BATCH - 1):
            there = pl.ds(pl.multiple_of((count + i) * BLOCK, BLOCK), BLOCK)
            key_value[there, :] = lines[0][:BLOCK, :]
            limit_at[count + i] = jnp.int32(-2 * BLOCK)

        rows = query[:, query_core, :, query_yh].reshape(GQ * BLOCK, HD)
        numer[...] = jnp.zeros_like(numer)
        total[...] = jnp.zeros_like(total)

        def batch(at, carry):
            first = at * BATCH
            limits = [limit_at[first + i] for i in range(BATCH)]
            there = pl.ds(pl.multiple_of(first * BLOCK, BATCH * BLOCK), BATCH * BLOCK)
            scores = lax.dot_general(
                rows,
                key_value[there, :HD],
                (((1,), (1,)), ((), ())),
                preferred_element_type=f32,
            )
            raised = jnp.exp2(scores * (math.log2(math.e) / math.sqrt(HD)))
            parts = [
                jnp.where(ahead <= limits[i], raised[:, i * BLOCK : (i + 1) * BLOCK], 0.0)
                for i in range(BATCH)
            ]
            total[...] += (parts[0] + parts[1]) + (parts[2] + parts[3])
            weights = jnp.concatenate([p.astype(bf16) for p in parts], axis=1)
            numer[...] += jnp.dot(weights, key_value[there, HD:], preferred_element_type=f32)
            return carry

        lax.fori_loop(0, (count + BATCH - 1) // BATCH, batch, 0)

        denom = jnp.sum(total[...], axis=1, keepdims=True)
        tail = jnp.zeros((BLOCK, HD), f32)
        for head in range(GQ):
            at = slice(head * BLOCK, (head + 1) * BLOCK)
            tail = jnp.where(lane == head, denom[at], tail)
            out[:, head * HD : (head + 1) * HD] = numer[at].astype(out.dtype)
        out[:, GQ * HD :] = tail if out.dtype == f32 else two_words(tail)


def two_words(denom):
    high = denom.astype(bf16).astype(f32)
    return (high + pltpu.roll(denom - high, LOW, 1)).astype(bf16)


def attend(remote, masks, query, lines, after=()):
    tok = query.shape[-2]
    rows = GQ * tok
    blocks = len(OFFSETS) * ZH + BATCH - 1
    in_vmem = pl.BlockSpec(memory_space=pltpu.VMEM)
    return pl.pallas_call(
        functools.partial(attend_kernel, remote),
        in_specs=[pl.BlockSpec(memory_space=pltpu.SMEM)]
        + [in_vmem] * (1 + len(lines))
        + [pl.BlockSpec(memory_space=pl.ANY)] * len(after),
        scratch_shapes=[
            pltpu.VMEM((blocks * BLOCK, 2 * HD), bf16),
            pltpu.VMEM((rows, HD), f32),
            pltpu.VMEM((rows, BLOCK), f32),
            pltpu.SMEM((blocks,), jnp.int32),
        ],
        out_shape=(
            jax.ShapeDtypeStruct((tok, WIDTH), f32 if remote else bf16),
            jax.ShapeDtypeStruct((tok, WIDTH), f32),
        ),
        compiler_params=params(),
        cost_estimate=pl.CostEstimate(
            flops=4 * CORE * rows * blocks * BLOCK * HD,
            bytes_accessed=4 * blocks * BLOCK * HD,
            transcendentals=CORE * rows * blocks * BLOCK,
        ),
        name="attend_remote" if remote else "attend_local",
    )(masks, query, *lines, *after)


def fold_kernel(own, both, out):
    got = both.at[1 - lax.axis_index("c")]
    out[:, : GQ * HD] = (own[:, : GQ * HD] + got[:, : GQ * HD]).astype(bf16)
    out[:, GQ * HD :] = two_words(own[:, GQ * HD :] + got[:, GQ * HD :])


def fold(own, both):
    return pl.pallas_call(
        fold_kernel,
        out_shape=jax.ShapeDtypeStruct(own.shape, bf16),
        compiler_params=params(),
        name="fold",
    )(own, both)


def combine_kernel(own, both, far, out):
    got = both.at[1 - lax.axis_index("c")]
    tail = own[:, GQ * HD :] + got[:, GQ * HD :].astype(f32) + far[:, GQ * HD :].astype(f32)
    for head in range(GQ):
        at = slice(head * HD, (head + 1) * HD)
        numer = own[:, at] + got[:, at].astype(f32) + far[:, at].astype(f32)
        denom = tail[:, head : head + 1] + tail[:, head + LOW : head + LOW + 1]
        out[:, at] = (numer / denom).astype(bf16)


def combine(own, both, far):
    return pl.pallas_call(
        combine_kernel,
        out_shape=jax.ShapeDtypeStruct((own.shape[0], GQ * HD), bf16),
        compiler_params=params(),
        name="combine",
    )(own, both, far)


def local(hidden, qkv_weight, query_gain, key_gain, positions, block_mask):
    tok, depth = hidden.shape
    share = qkv_weight.shape[0]
    yh, zh, zl, core = (lax.axis_index(a) for a in DP)
    with jax.named_scope("weights"):
        got = lax.all_to_all(pack(qkv_weight), ("yh", "x", "yl"), 0, 0)
        got, sent = lax.optimization_barrier((got, hidden))
        far = swap(sent, "yh")
        rows, wide = KV * share, PAIR * HD
        q_rows = got[:, :, :wide].reshape(YH * rows, wide)
        kv_rows = lax.dynamic_index_in_dim(
            got.reshape(YH, KV, share, 2 * wide), yh, 0, keepdims=False
        )[:, :, wide:].reshape(rows, wide)
        q_weight = lax.all_gather(q_rows, Z + ("c",), axis=0, tiled=False)
        q_weight = q_weight.reshape(NZ, CORE, YH, rows, wide)
        kv_weight = lax.all_gather(
            kv_rows, Z + ("c",), axis=0, tiled=True, axis_index_groups=ALTERNATE
        )

    hiddens = (hidden, far)

    inverse = 1000000.0 ** (-(jnp.arange(HD // 2, dtype=f32) * 2.0) / HD)
    own = []
    for rel in range(YH):
        first = ((yh ^ rel) * NZ + zh * ZL + zl) * CORE + core
        own.append(lax.dynamic_slice_in_dim(positions, first * tok, tok, 0))
    angles = jnp.stack(own).astype(f32)[:, :, None] * inverse
    cosine, sine = jnp.cos(angles), jnp.sin(angles)
    cosine = jnp.concatenate([cosine, cosine], axis=-1)
    sine = jnp.concatenate([-sine, sine], axis=-1)

    with jax.named_scope("keys_values"):
        keep, send = kv_partial(hiddens, kv_weight, swap(kv_weight, "c"))
        sent = lax.all_gather(send, "yh", axis=0, tiled=False)
        keys, values, both = kv_finish(
            keep, sent, key_gain.reshape(1, HD), cosine, sine
        )
        line = lax.all_gather(both, "zh", axis=0, tiled=True)
        line, q_weight = lax.optimization_barrier((line, q_weight))
        across = from_z_both(line, 2)
        gathered = (line, from_z(line, 1), from_z(line, -1), across)

    with jax.named_scope("queries"):
        query = q_project(hiddens, q_weight, query_gain.reshape(1, HD), cosine, sine)
        query = lax.all_gather(query, ("yh", "c"), axis=0, tiled=False)
        query = query.reshape(YH, CORE, PAIR, YH, tok, HD)

    masks = block_mask.reshape(YH, NZ, CORE, block_mask.shape[1])
    masks = lax.dynamic_index_in_dim(masks, zh * ZL + zl, 1, keepdims=False)
    masks = masks.reshape(GROUP, block_mask.shape[1])

    with jax.named_scope("context"):
        peer, own = attend(True, masks, query, gathered)
        both = lax.all_gather(peer, "c", axis=0, tiled=False)
        folded = fold(own, both)
        far_part = lax.ppermute(folded, "yh", [(0, 1)])
        peer, own = attend(False, masks, query, gathered, (folded,))
        both = lax.all_gather(peer, "c", axis=0, tiled=False)
        context = combine(own, both, far_part)
    return keys, values, context


def solution(mesh):
    fine = Mesh(mesh.devices.reshape(YH, ZH, ZL, CORE, X, YL), DP[:3] + ("c",) + TENSOR)
    return jax.shard_map(
        local,
        mesh=fine,
        in_specs=(P(DP, None), P(DP + TENSOR, None), P(), P(), P(), P()),
        out_specs=(P(DP, TENSOR), P(DP, TENSOR), P(DP, TENSOR)),
        check_vma=False,
    )
```

```python
import functools
import math

import jax
import jax.numpy as jnp
from jax import lax
from jax.experimental import pallas as pl
from jax.experimental.pallas import tpu as pltpu
from jax.sharding import Mesh, PartitionSpec as P

HD = 128
BLOCK = 128
GQ = 4
PAIR = 2
KV = 8
YH, ZH, ZL, CORE, X, YL = 2, 4, 4, 2, 4, 2
NZ = ZH * ZL
GROUP = YH * CORE
DP = ("yh", "zh", "zl", "c")
TENSOR = ("x", "yl")
Z = ("zh", "zl")
bf16 = jnp.bfloat16
f32 = jnp.float32


ALTERNATE = [[z * CORE + (z + first) % CORE for z in range(NZ)] for first in range(CORE)]


def params():
    return pltpu.CompilerParams(vmem_limit_bytes=24 * 1024 * 1024)


def swap(inputs, axis):
    return lax.ppermute(inputs, axis, [(0, 1), (1, 0)])


def from_z(inputs, offset):
    return lax.ppermute(inputs, Z, [(i, (i - offset) % NZ) for i in range(NZ)])


def from_z_both(inputs, offset):
    pairs = [
        (i * CORE + core, (i - (1 - 2 * core) * offset) % NZ * CORE + core)
        for i in range(NZ)
        for core in range(CORE)
    ]
    return lax.ppermute(inputs, Z + ("c",), pairs)


def norm_rope(inputs, gain, cosine, sine):
    meansq = jnp.mean(inputs * inputs, axis=-1, keepdims=True)
    normed = inputs * lax.rsqrt(meansq + 1e-06) * gain
    return normed * cosine + pltpu.roll(normed, HD // 2, 1) * sine


def pack_kernel(weight, out):
    for yh in range(YH):
        for head in range(KV):
            first = head * (GQ + 2)
            for i, slot in enumerate((first + yh * PAIR, first + GQ)):
                out[yh * KV + head, :, i * PAIR * HD : (i + 1) * PAIR * HD] = weight[
                    :, slot * HD : (slot + PAIR) * HD
                ]


def pack(weight):
    return pl.pallas_call(
        pack_kernel,
        out_shape=jax.ShapeDtypeStruct(
            (YH * KV, weight.shape[0], 2 * PAIR * HD), weight.dtype
        ),
        compiler_params=params(),
        name="pack",
    )(weight)


def kv_partial_kernel(h0, h1, mine, other, keep, send, weight):
    core = lax.axis_index("c")
    pairs, _, _, share, wide = weight.shape
    nz = 2 * pairs
    half = nz * CORE * share
    even = lax.rem(core + lax.axis_index("zl"), 2)
    for source, first in ((mine, even), (other, 1 - even)):
        chunks = source[...].reshape(nz // 2, 2, share, wide)
        weight[:, 0, first] = chunks[:, 0]
        weight[:, 1, 1 - first] = chunks[:, 1]
    columns = pl.ds(pl.multiple_of(lax.axis_index("yh") * half, half), half)
    whole = weight[...].reshape(half, wide)
    for rows, out in ((h0, keep), (h1, send)):
        total = jnp.dot(rows[:, columns], whole, preferred_element_type=f32)
        out[...] = total.astype(out.dtype)


def kv_partial(hiddens, mine, other):
    tok = hiddens[0].shape[0]
    shape = (tok, 2 * HD)
    return pl.pallas_call(
        kv_partial_kernel,
        out_shape=(jax.ShapeDtypeStruct(shape, f32), jax.ShapeDtypeStruct(shape, bf16)),
        scratch_shapes=[pltpu.VMEM((NZ // 2, 2, CORE, mine.shape[0] // NZ, mine.shape[1]), bf16)],
        compiler_params=params(),
        name="kv_partial",
    )(*hiddens, mine, other)


def kv_finish_kernel(keep, sent, gain, cosine, sine, keys, values, both):
    total = keep[...] + sent[1 - lax.axis_index("yh")].astype(f32)
    key = norm_rope(total[:, :HD], gain[...], cosine[0], sine[0]).astype(bf16)
    value = total[:, HD:].astype(bf16)
    keys[...] = key
    values[...] = value
    both[:, :HD] = key
    both[:, HD:] = value


def kv_finish(keep, sent, gain, cosine, sine):
    tok = keep.shape[0]
    return pl.pallas_call(
        kv_finish_kernel,
        out_shape=(
            jax.ShapeDtypeStruct((tok, HD), bf16),
            jax.ShapeDtypeStruct((tok, HD), bf16),
            jax.ShapeDtypeStruct((tok, 2 * HD), bf16),
        ),
        compiler_params=params(),
        name="kv_finish",
    )(keep, sent, gain, cosine, sine)


def q_project_kernel(h0, h1, gain, cosine, sine, weight, out):
    yh = lax.axis_index("yh")
    half = h0.shape[1] // YH
    totals = [None] * YH
    for i in range(YH):
        columns = weight[:, :, i].reshape(half, PAIR * HD)
        for rel, rows in enumerate((h0, h1)):
            part = jnp.dot(
                rows[:, i * half : (i + 1) * half], columns, preferred_element_type=f32
            )
            totals[rel] = part if i == 0 else totals[rel] + part
    for rel, total in enumerate(totals):
        for head in range(PAIR):
            out[head, yh ^ rel] = norm_rope(
                total[:, head * HD : (head + 1) * HD], gain[...], cosine[rel], sine[rel]
            ).astype(bf16)


def q_project(hiddens, weight, gain, cosine, sine):
    tok = hiddens[0].shape[0]
    return pl.pallas_call(
        q_project_kernel,
        out_shape=jax.ShapeDtypeStruct((PAIR, YH, tok, HD), bf16),
        compiler_params=params(),
        name="q_project",
    )(*hiddens, gain, cosine, sine, weight)


OFFSETS = (0, 1, -1, 2)
BATCH = 4
WIDTH = (GQ + 1) * HD
LOW = 64


def attend_kernel(remote, masks, query, *refs):
    lines = refs[: len(OFFSETS)]
    peer, own, key_value, numer, total, limit_at = refs[-6:]
    yh, zh, zl, core = (lax.axis_index(a) for a in DP)
    query_yh = 1 - yh if remote else yh
    ahead = lax.broadcasted_iota(jnp.int32, (GQ * BLOCK, BLOCK), 1) - lax.rem(
        lax.broadcasted_iota(jnp.int32, (GQ * BLOCK, BLOCK), 0), BLOCK
    )
    lane = lax.broadcasted_iota(jnp.int32, (BLOCK, HD), 1)
    for query_core, out in ((1 - core, peer), (core, own)):
        query_block = query_yh * (NZ * CORE) + (zh * ZL + zl) * CORE + query_core
        count = jnp.int32(0)
        for i, offset in enumerate(OFFSETS):
            for j in range(ZH):
                z_at = j * ZL + lax.rem(zl + (offset + ZL), ZL)
                key_block = yh * (NZ * CORE) + z_at * CORE + core
                live = (masks[query_yh * CORE + query_core, key_block] == 1) & (key_block <= query_block)

                @pl.when(live)
                def _(i=i, j=j, count=count, key_block=key_block, query_block=query_block):
                    there = pl.ds(pl.multiple_of(count * BLOCK, BLOCK), BLOCK)
                    key_value[there, :] = lines[i][j * BLOCK : (j + 1) * BLOCK, :]
                    limit_at[count] = jnp.where(key_block == query_block, 0, 2 * BLOCK)

                count = count + live.astype(jnp.int32)
        for i in range(BATCH - 1):
            there = pl.ds(pl.multiple_of((count + i) * BLOCK, BLOCK), BLOCK)
            key_value[there, :] = lines[0][:BLOCK, :]
            limit_at[count + i] = jnp.int32(-2 * BLOCK)

        rows = query[:, query_core, :, query_yh].reshape(GQ * BLOCK, HD)
        numer[...] = jnp.zeros_like(numer)
        total[...] = jnp.zeros_like(total)

        def batch(at, carry):
            first = at * BATCH
            limits = [limit_at[first + i] for i in range(BATCH)]
            there = pl.ds(pl.multiple_of(first * BLOCK, BATCH * BLOCK), BATCH * BLOCK)
            scores = lax.dot_general(
                rows,
                key_value[there, :HD],
                (((1,), (1,)), ((), ())),
                preferred_element_type=f32,
            )
            raised = jnp.exp2(scores * (math.log2(math.e) / math.sqrt(HD)))
            parts = [
                jnp.where(ahead <= limits[i], raised[:, i * BLOCK : (i + 1) * BLOCK], 0.0)
                for i in range(BATCH)
            ]
            total[...] += (parts[0] + parts[1]) + (parts[2] + parts[3])
            weights = jnp.concatenate([p.astype(bf16) for p in parts], axis=1)
            numer[...] += jnp.dot(weights, key_value[there, HD:], preferred_element_type=f32)
            return carry

        lax.fori_loop(0, (count + BATCH - 1) // BATCH, batch, 0)

        denom = jnp.sum(total[...], axis=1, keepdims=True)
        tail = jnp.zeros((BLOCK, HD), f32)
        for head in range(GQ):
            at = slice(head * BLOCK, (head + 1) * BLOCK)
            tail = jnp.where(lane == head, denom[at], tail)
            out[:, head * HD : (head + 1) * HD] = numer[at].astype(out.dtype)
        out[:, GQ * HD :] = tail if out.dtype == f32 else two_words(tail)


def two_words(denom):
    high = denom.astype(bf16).astype(f32)
    return (high + pltpu.roll(denom - high, LOW, 1)).astype(bf16)


def attend(remote, masks, query, lines, after=()):
    tok = query.shape[-2]
    rows = GQ * tok
    blocks = len(OFFSETS) * ZH + BATCH - 1
    in_vmem = pl.BlockSpec(memory_space=pltpu.VMEM)
    return pl.pallas_call(
        functools.partial(attend_kernel, remote),
        in_specs=[pl.BlockSpec(memory_space=pltpu.SMEM)]
        + [in_vmem] * (1 + len(lines))
        + [pl.BlockSpec(memory_space=pl.ANY)] * len(after),
        scratch_shapes=[
            pltpu.VMEM((blocks * BLOCK, 2 * HD), bf16),
            pltpu.VMEM((rows, HD), f32),
            pltpu.VMEM((rows, BLOCK), f32),
            pltpu.SMEM((blocks,), jnp.int32),
        ],
        out_shape=(
            jax.ShapeDtypeStruct((tok, WIDTH), f32 if remote else bf16),
            jax.ShapeDtypeStruct((tok, WIDTH), f32),
        ),
        compiler_params=params(),
        cost_estimate=pl.CostEstimate(
            flops=4 * CORE * rows * blocks * BLOCK * HD,
            bytes_accessed=4 * blocks * BLOCK * HD,
            transcendentals=CORE * rows * blocks * BLOCK,
        ),
        name="attend_remote" if remote else "attend_local",
    )(masks, query, *lines, *after)


def fold_kernel(own, both, out):
    got = both.at[1 - lax.axis_index("c")]
    out[:, : GQ * HD] = (own[:, : GQ * HD] + got[:, : GQ * HD]).astype(bf16)
    out[:, GQ * HD :] = two_words(own[:, GQ * HD :] + got[:, GQ * HD :])


def fold(own, both):
    return pl.pallas_call(
        fold_kernel,
        out_shape=jax.ShapeDtypeStruct(own.shape, bf16),
        compiler_params=params(),
        name="fold",
    )(own, both)


def combine_kernel(own, both, far, out):
    got = both.at[1 - lax.axis_index("c")]
    tail = own[:, GQ * HD :] + got[:, GQ * HD :].astype(f32) + far[:, GQ * HD :].astype(f32)
    for head in range(GQ):
        at = slice(head * HD, (head + 1) * HD)
        numer = own[:, at] + got[:, at].astype(f32) + far[:, at].astype(f32)
        denom = tail[:, head : head + 1] + tail[:, head + LOW : head + LOW + 1]
        out[:, at] = (numer / denom).astype(bf16)


def combine(own, both, far):
    return pl.pallas_call(
        combine_kernel,
        out_shape=jax.ShapeDtypeStruct((own.shape[0], GQ * HD), bf16),
        compiler_params=params(),
        name="combine",
    )(own, both, far)


def local(hidden, qkv_weight, query_gain, key_gain, positions, block_mask):
    tok, depth = hidden.shape
    share = qkv_weight.shape[0]
    yh, zh, zl, core = (lax.axis_index(a) for a in DP)
    with jax.named_scope("weights"):
        got = lax.all_to_all(pack(qkv_weight), ("yh", "x", "yl"), 0, 0)
        got, sent = lax.optimization_barrier((got, hidden))
        far = swap(sent, "yh")
        rows, wide = KV * share, PAIR * HD
        q_rows = got[:, :, :wide].reshape(YH * rows, wide)
        kv_rows = lax.dynamic_index_in_dim(
            got.reshape(YH, KV, share, 2 * wide), yh, 0, keepdims=False
        )[:, :, wide:].reshape(rows, wide)
        q_weight = lax.all_gather(q_rows, Z + ("c",), axis=0, tiled=False)
        q_weight = q_weight.reshape(NZ, CORE, YH, rows, wide)
        kv_weight = lax.all_gather(
            kv_rows, Z + ("c",), axis=0, tiled=True, axis_index_groups=ALTERNATE
        )

    hiddens = (hidden, far)

    inverse = 1000000.0 ** (-(jnp.arange(HD // 2, dtype=f32) * 2.0) / HD)
    own = []
    for rel in range(YH):
        first = ((yh ^ rel) * NZ + zh * ZL + zl) * CORE + core
        own.append(lax.dynamic_slice_in_dim(positions, first * tok, tok, 0))
    angles = jnp.stack(own).astype(f32)[:, :, None] * inverse
    cosine, sine = jnp.cos(angles), jnp.sin(angles)
    cosine = jnp.concatenate([cosine, cosine], axis=-1)
    sine = jnp.concatenate([-sine, sine], axis=-1)

    with jax.named_scope("keys_values"):
        keep, send = kv_partial(hiddens, kv_weight, swap(kv_weight, "c"))
        sent = lax.all_gather(send, "yh", axis=0, tiled=False)
        keys, values, both = kv_finish(
            keep, sent, key_gain.reshape(1, HD), cosine, sine
        )
        line = lax.all_gather(both, "zh", axis=0, tiled=True)
        line, q_weight = lax.optimization_barrier((line, q_weight))
        across = from_z_both(line, 2)
        gathered = (line, from_z(line, 1), from_z(line, -1), across)

    with jax.named_scope("queries"):
        query = q_project(hiddens, q_weight, query_gain.reshape(1, HD), cosine, sine)
        query = lax.all_gather(query, ("yh", "c"), axis=0, tiled=False)
        query = query.reshape(YH, CORE, PAIR, YH, tok, HD)

    masks = block_mask.reshape(YH, NZ, CORE, block_mask.shape[1])
    masks = lax.dynamic_index_in_dim(masks, zh * ZL + zl, 1, keepdims=False)
    masks = masks.reshape(GROUP, block_mask.shape[1])

    with jax.named_scope("context"):
        peer, own = attend(True, masks, query, gathered)
        both = lax.all_gather(peer, "c", axis=0, tiled=False)
        folded = fold(own, both)
        far_part = lax.ppermute(folded, "yh", [(0, 1)])
        peer, own = attend(False, masks, query, gathered, (folded,))
        both = lax.all_gather(peer, "c", axis=0, tiled=False)
        context = combine(own, both, far_part)
    return keys, values, context


def solution(mesh):
    fine = Mesh(mesh.devices.reshape(YH, ZH, ZL, CORE, X, YL), DP[:3] + ("c",) + TENSOR)
    return jax.shard_map(
        local,
        mesh=fine,
        in_specs=(P(DP, None), P(DP + TENSOR, None), P(), P(), P(), P()),
        out_specs=(P(DP, TENSOR), P(DP, TENSOR), P(DP, TENSOR)),
        check_vma=False,
    )
```
